1024 devices in a mesh: replica: 64 (over y, z_lo, core), tensor: 16 (over x, z_hi).
Axes of the slice: x: 4, y: 8, z: 16 (z_hi: 4, z_lo: 4; z = z_hi * 4 + z_lo), core: 2. Of those that a mesh axis runs over, the one named last changes fastest.
Arguments:
- attention_heads_output: bfloat16 [16384, 8192], P('replica', 'tensor'), may hold values from -6 to 6
- output_projection_weight: bfloat16 [8192, 8192], P('tensor'), may hold values from -0.0625 to 0.0625
- adapter_down_factors: bfloat16 [512, 64, 8192], P(None, 'replica', 'tensor'), may hold values from -0.0625 to 0.0625
- adapter_up_factors: bfloat16 [512, 64, 8192], P(None, 'replica', 'tensor'), may hold values from -0.75 to 0.75
- group_working_adapters: int32 [64, 8], replicated, may hold values from 0 to 511, as said below
- adapter_store_row: int32 [512], replicated, may hold values from 0 to 511, each once
- request_working_slot: int32 [16384], P('replica'), may hold values from 0 to 7
Outputs:
- projected: bfloat16 [16384, 8192], P('replica', 'tensor')
The draws below stay inside these ranges and needn't reach their ends.
Inputs may be any that keep to these rules, and one draw needn't show every extreme that they name: `group_working_adapters`: the 8 ids of one group are distinct. `adapter_store_row`: each adapter has its own row.
All inputs are finite; a program needn't handle non-finite values.
Results may differ from the reference program's by a relative error of at most 0.0028.
Values may be sent and summed in bfloat16 or wider, within the bound.
No kernel may reach another device: no remote copies, remote signals or barrier semaphores. Data moves between devices by JAX's collectives and lax.ppermute only.
A program may use at most 64 MiB of HBM per device.

```python
import math
import jax
import jax.numpy as jnp
import numpy as np
from jax import lax

MODEL_WIDTH = 8192
ADAPTER_RANK = 64
REQ = 256
STORE_ADAPTERS = 512
WORKING_SLOTS = 8
GROUPS = 64
TOKENS = 16384


def draw_group_working_adapters(key, part):
    key = jax.random.fold_in(key, 11)
    keys = jax.random.split(key, GROUPS)

    def single(one_key):
        return jax.random.permutation(one_key, STORE_ADAPTERS)[:WORKING_SLOTS]
    return jax.vmap(single)(keys).astype(jnp.int32)


def set_ends(values, rng, low, top_value):
    place = [jax.random.randint(jax.random.fold_in(rng, axis), (), 0, length) for axis, length in enumerate(values.shape)]
    main_axis = values.shape.index(max(values.shape))
    beside = place[:main_axis] + [(place[main_axis] + 1) % values.shape[main_axis]] + place[main_axis + 1:]
    return values.at[tuple(place)].set(low).at[tuple(beside)].set(top_value)


def block_levels(key, dims, shards, least, top_value):
    factor_of = 1.0
    for dim, blocks in shards:
        draws = jax.random.uniform(jax.random.fold_in(jax.random.fold_in(key, 6), dim), (blocks,), jnp.float32, least / len(shards), top_value / len(shards))
        factor_of = factor_of * jnp.repeat(jnp.exp(draws), dims[dim] // blocks).reshape((-1,) + (1,) * (len(dims) - 1 - dim))
    return factor_of


def rank_bounds(count, slope):
    loads = [(1 << 20) // math.isqrt(standing ** slope) + 1 for standing in range(1, count + 1)]
    deviation = 1 + sum(loads) // (1 << 30)
    return np.cumsum(np.array([max(1, weight // deviation) for weight in loads]))


def skewed_ids(rng, extent, amount, lean):
    table = rank_bounds(amount, lean)
    lot = jax.random.randint(jax.random.fold_in(rng, 1), extent, 0, int(table[amount - 1]))
    rank = jnp.searchsorted(jnp.asarray(table, jnp.int32), lot, side="right")
    return jax.random.permutation(jax.random.fold_in(rng, 2), amount)[rank].astype(jnp.int32)


def bell_draw(own_key, dims, deviation, reach, shards=(), kind=jnp.bfloat16):
    entries = jax.random.normal(own_key, dims, jnp.float32) * deviation
    if len(shards) > 0:
        entries = block_levels(own_key, dims, shards, -0.22, 0.18) * entries
    return jnp.clip(entries, min=-reach, max=reach).astype(kind)


def setup_inputs(seed: int = 0) -> dict:
    seeds = jax.random.split(jax.random.key(seed), 8)
    return {
        "attention_heads_output": bell_draw(seeds[0], (TOKENS, MODEL_WIDTH), 1.0, 6.0, ((0, 64), (1, 16))),
        "output_projection_weight": bell_draw(seeds[1], (MODEL_WIDTH, MODEL_WIDTH), MODEL_WIDTH ** -0.5, 0.0625, ((0, 16),)),
        "adapter_down_factors": bell_draw(seeds[2], (STORE_ADAPTERS, ADAPTER_RANK, MODEL_WIDTH), MODEL_WIDTH ** -0.5, 0.0625, ((1, 64), (2, 16))),
        "adapter_up_factors": bell_draw(seeds[3], (STORE_ADAPTERS, ADAPTER_RANK, MODEL_WIDTH), ADAPTER_RANK ** -0.5, 0.75, ((1, 64), (2, 16))),
        "group_working_adapters": draw_group_working_adapters(jax.random.fold_in(seeds[7], 71), 0),
        "adapter_store_row": jax.random.permutation(seeds[5], STORE_ADAPTERS).astype(jnp.int32),
        "request_working_slot": set_ends(skewed_ids(seeds[6], (TOKENS,), WORKING_SLOTS, 2), jax.random.fold_in(seeds[6], 3), 0, WORKING_SLOTS - 1).astype(jnp.int32),
    }


ADAPTER_SCALE = 0.5


def reference(attention_heads_output, output_projection_weight, adapter_down_factors, adapter_up_factors, group_working_adapters, adapter_store_row, request_working_slot):
    def one_group(packed):
        block, slot_ids, adapter_ids = packed
        chosen_adapter_index = jnp.take(adapter_store_row, adapter_ids, axis=0).astype(jnp.int32)
        down_factor_rows = jnp.take(adapter_down_factors, chosen_adapter_index, axis=0).reshape(WORKING_SLOTS * ADAPTER_RANK, MODEL_WIDTH)
        up_factor_rows = jnp.take(adapter_up_factors, chosen_adapter_index, axis=0).reshape(WORKING_SLOTS * ADAPTER_RANK, MODEL_WIDTH)
        selector = (slot_ids[:, None] == jnp.arange(WORKING_SLOTS, dtype=jnp.int32)[None, :]).astype(jnp.float32)
        base_projection = jnp.dot(block, output_projection_weight, preferred_element_type=jnp.float32)
        all_ranks = lax.dot_general(block, down_factor_rows, (((1,), (1,)), ((), ())), preferred_element_type=jnp.float32)
        rank_part = jnp.sum(all_ranks.reshape(REQ, WORKING_SLOTS, ADAPTER_RANK) * selector[:, :, None], axis=1)
        rounded = rank_part.astype(jnp.bfloat16)
        expanded = (rounded[:, None, :] * selector[:, :, None].astype(jnp.bfloat16)).reshape(REQ, WORKING_SLOTS * ADAPTER_RANK)
        adapter_contribution = jnp.dot(expanded, up_factor_rows, preferred_element_type=jnp.float32)
        return (base_projection + ADAPTER_SCALE * adapter_contribution).astype(jnp.bfloat16)

    result = lax.map(one_group, (attention_heads_output.reshape(GROUPS, REQ, MODEL_WIDTH), request_working_slot.reshape(GROUPS, REQ), group_working_adapters))
    return result.reshape(TOKENS, MODEL_WIDTH)
```

```python
import jax
import jax.numpy as jnp
from jax import lax
from jax.sharding import Mesh, PartitionSpec as P

ADAPTER_RANK = 64
WORKING_SLOTS = 8
ADAPTER_SCALE = 0.5
CHUNKS = ((2,), (1, 3), (0,))

f32 = jnp.float32
bf16 = jnp.bfloat16

REPLICA = ("y", "zl", "c")
TENSOR = ("x", "zh")


def fetch_adapters(down_store, up_store, working_adapters, store_row):
    groups = working_adapters.shape[0]
    adapters, _, features = down_store.shape
    ids = working_adapters.reshape(-1)
    is_adapter = ids[:, None] == lax.broadcasted_iota(jnp.int32, (ids.shape[0], adapters), 1)
    rows = jnp.sum(jnp.where(is_adapter, store_row[None, :], 0), axis=1)
    pick = (rows[:, None] == lax.broadcasted_iota(jnp.int32, (ids.shape[0], adapters), 1)).astype(bf16)
    down = jnp.dot(pick, down_store[:, 0, :], preferred_element_type=f32).astype(bf16)
    up = jnp.dot(pick, up_store[:, 0, :], preferred_element_type=f32).astype(bf16)
    outgoing = jnp.concatenate(
        [down.reshape(groups, WORKING_SLOTS, features), up.reshape(groups, WORKING_SLOTS, features)], axis=1
    )
    fetched = lax.all_to_all(outgoing, REPLICA, split_axis=0, concat_axis=0, tiled=True)
    fetched = fetched.transpose(1, 0, 2)
    down = fetched[:WORKING_SLOTS].reshape(WORKING_SLOTS * ADAPTER_RANK, features)
    up = fetched[WORKING_SLOTS:].reshape(WORKING_SLOTS * ADAPTER_RANK, features)
    return down, up


def sum_over_tensor(part):
    shape = part.shape
    pieces = part.reshape(16, -1, 128)
    pieces = lax.all_to_all(pieces, TENSOR, split_axis=0, concat_axis=0, tiled=True)
    own = jnp.sum(pieces, axis=0).astype(bf16)
    spread = jnp.broadcast_to(own[None], (16,) + own.shape)
    spread = lax.all_to_all(spread, TENSOR, split_axis=0, concat_axis=0, tiled=True)
    return spread.reshape(shape)


def shifted(value, axis, by):
    size = lax.axis_size(axis)
    return lax.ppermute(value, axis, [(i, (i + by) % size) for i in range(size)])


def body(x_block, weight, down_store, up_store, working_adapters, store_row, slot):
    rows, features = x_block.shape
    xs, zs = lax.axis_size("x"), lax.axis_size("zh")
    core, x_at, z_at = lax.axis_index("c"), lax.axis_index("x"), lax.axis_index("zh")
    half = features // 2

    swapped = jnp.concatenate([x_block[:, half:], x_block[:, :half]], axis=1)
    ordered = jnp.where(core == 0, x_block, swapped)
    blocks = [shifted(ordered, "x", by) for by in range(1, xs)]
    lhs_mine = jnp.concatenate([block[:, :half] for block in blocks], axis=1)
    lhs_other = jnp.concatenate([block[:, half:] for block in blocks], axis=1)

    down, up = fetch_adapters(down_store, up_store, working_adapters, store_row)
    selector = slot[:, None] == jnp.arange(WORKING_SLOTS, dtype=jnp.int32)[None, :]
    all_ranks = lax.dot_general(x_block, down, (((1,), (1,)), ((), ())), preferred_element_type=f32)
    rank_local = jnp.sum(
        all_ranks.reshape(rows, WORKING_SLOTS, ADAPTER_RANK) * selector.astype(f32)[:, :, None], axis=1
    )
    rounded = sum_over_tensor(rank_local)
    expanded = (rounded[:, None, :] * selector.astype(bf16)[:, :, None]).reshape(rows, WORKING_SLOTS * ADAPTER_RANK)

    def columns(x_by, z_by):
        return (lax.rem(x_at + x_by, xs) * zs + lax.rem(z_at + z_by, zs)) * features

    def weight_of(z_bys, x_by):
        return jnp.concatenate(
            [lax.dynamic_slice(weight, (core * half, columns(x_by, z_by)), (half, features)) for z_by in z_bys], axis=1
        )

    total = None
    for z_bys in CHUNKS:
        mine = jnp.concatenate([shifted(weight_of(z_bys, by), "x", by) for by in range(1, xs)], axis=0)
        other = shifted(mine, "c", 1)
        partial = jnp.dot(lhs_mine, mine, preferred_element_type=f32) + jnp.dot(
            lhs_other, other, preferred_element_type=f32
        )
        for k, z_by in enumerate(z_bys):
            own = lax.dynamic_slice(weight, (0, columns(0, z_by)), (features, features))
            part = partial[:, k * features:(k + 1) * features] + jnp.dot(x_block, own, preferred_element_type=f32)
            if z_by:
                part = shifted(part.astype(bf16), "zh", z_by).astype(f32)
            total = part if total is None else total + part
    term = jnp.dot(expanded, up, preferred_element_type=f32)
    return (total + ADAPTER_SCALE * term).astype(bf16)


def solution(mesh):
    fine = Mesh(mesh.devices.reshape(8, 4, 2, 4, 4), ("y", "zl", "c", "x", "zh"))
    in_specs = (
        P(REPLICA, TENSOR),
        P(TENSOR, None),
        P(None, REPLICA, TENSOR),
        P(None, REPLICA, TENSOR),
        P(),
        P(),
        P(REPLICA),
    )
    return jax.shard_map(body, mesh=fine, in_specs=in_specs, out_specs=P(REPLICA, TENSOR), check_vma=False)
```

```python
import jax
import jax.numpy as jnp
from jax import lax
from jax.sharding import Mesh, PartitionSpec as P

ADAPTER_RANK = 64
WORKING_SLOTS = 8
ADAPTER_SCALE = 0.5

f32 = jnp.float32
bf16 = jnp.bfloat16

REPLICA = ("y", "zl", "c")
TENSOR = ("x", "zh")


def after(value, *earlier):
    return lax.optimization_barrier((value,) + earlier)[0]


def picking(working_adapters, store_row, adapters):
    ids = working_adapters.reshape(-1)
    places = lax.broadcasted_iota(jnp.int32, (ids.shape[0], adapters), 1)
    rows = jnp.sum(jnp.where(ids[:, None] == places, store_row[None, :], 0), axis=1)
    return (rows[:, None] == places).astype(bf16)


def fetch(pick, store):
    features = store.shape[2]
    out = jnp.dot(pick, store[:, 0, :], preferred_element_type=f32).astype(bf16)
    out = out.reshape(-1, WORKING_SLOTS, features)
    fetched = lax.all_to_all(out, REPLICA, split_axis=0, concat_axis=0, tiled=True)
    return fetched.transpose(1, 0, 2).reshape(WORKING_SLOTS * ADAPTER_RANK, features)


def sum_over_tensor(part):
    shape = part.shape
    pieces = part.reshape(16, -1, 128)
    pieces = lax.all_to_all(pieces, TENSOR, split_axis=0, concat_axis=0, tiled=True)
    own = jnp.sum(pieces, axis=0).astype(bf16)
    spread = jnp.broadcast_to(own[None], (16,) + own.shape)
    spread = lax.all_to_all(spread, TENSOR, split_axis=0, concat_axis=0, tiled=True)
    return spread.reshape(shape)


def shifted(value, axis, by):
    size = lax.axis_size(axis)
    return lax.ppermute(value, axis, [(i, (i + by) % size) for i in range(size)])


def body(x_block, weight, down_store, up_store, working_adapters, store_row, slot):
    rows, features = x_block.shape
    xs, zs = lax.axis_size("x"), lax.axis_size("zh")
    core, x_at, z_at = lax.axis_index("c"), lax.axis_index("x"), lax.axis_index("zh")
    half = features // 2

    def columns(x_by, z_by):
        return (lax.rem(x_at + x_by, xs) * zs + lax.rem(z_at + z_by, zs)) * features

    def weight_of(source, x_by, z_by, c_by=0):
        return lax.dynamic_slice(source, (lax.rem(core + c_by, 2) * half, columns(x_by, z_by)), (half, features))

    def product(mine, other, z_bys, w):
        partial = jnp.dot(lhs_mine, mine, preferred_element_type=f32) + jnp.dot(
            lhs_other, other, preferred_element_type=f32
        )
        parts = []
        for k, z_by in enumerate(z_bys):
            own = lax.dynamic_slice(w, (0, columns(0, z_by)), (features, features))
            own = jnp.dot(x_block, own, preferred_element_type=f32)
            parts.append(partial[:, k * features:(k + 1) * features] + own)
        return parts

    pick = picking(working_adapters, store_row, down_store.shape[0])
    down = fetch(pick, down_store)

    swapped = jnp.concatenate([x_block[:, half:], x_block[:, :half]], axis=1)
    ordered = jnp.where(core == 0, x_block, swapped)
    got = [shifted(jnp.concatenate([ordered, weight_of(weight, by, 2)], axis=0), "x", by) for by in range(1, xs)]
    selector = slot[:, None] == jnp.arange(WORKING_SLOTS, dtype=jnp.int32)[None, :]
    all_ranks = lax.dot_general(x_block, down, (((1,), (1,)), ((), ())), preferred_element_type=f32)
    rank_local = jnp.sum(
        all_ranks.reshape(rows, WORKING_SLOTS, ADAPTER_RANK) * selector.astype(f32)[:, :, None], axis=1
    )
    lhs_mine = jnp.concatenate([block[:rows, :half] for block in got], axis=1)
    lhs_other = jnp.concatenate([block[:rows, half:] for block in got], axis=1)
    far_mine = jnp.concatenate([block[rows:] for block in got], axis=0)
    (far,) = product(far_mine, shifted(far_mine, "c", 1), (2,), weight)
    far = far.astype(bf16)
    far_sum = shifted(far, "zh", 2)
    rounded = sum_over_tensor(rank_local)
    expanded = (rounded[:, None, :] * selector.astype(bf16)[:, :, None]).reshape(rows, WORKING_SLOTS * ADAPTER_RANK)
    near_weight = after(weight, far)
    near = [
        shifted(jnp.concatenate([weight_of(near_weight, by, 1), weight_of(near_weight, by, 3)], axis=1), "x", by)
        for by in range(1, xs)
    ]

    near_mine = after(jnp.concatenate(near, axis=0), far_sum, rounded)
    up_part, down_part = product(near_mine, shifted(near_mine, "c", 1), (1, 3), weight)
    up_part, down_part = up_part.astype(bf16), down_part.astype(bf16)
    up_sum = shifted(up_part, "zh", 1)
    down_sum = shifted(down_part, "zh", 3)
    own_weight = after(weight, up_part, down_part)
    home = [
        shifted(
            jnp.concatenate([weight_of(own_weight, by, 0), weight_of(own_weight, by, 0, 1)], axis=1), "x", by
        )
        for by in range(1, xs)
    ]

    up = fetch(after(pick, rounded), up_store)
    home = after(jnp.concatenate(home, axis=0), up_sum, down_sum)
    (total,) = product(home[:, :features], home[:, features:], (0,), weight)
    total = total + far_sum.astype(f32) + up_sum.astype(f32) + down_sum.astype(f32)
    term = jnp.dot(expanded, up, preferred_element_type=f32)
    return (total + ADAPTER_SCALE * term).astype(bf16)


def solution(mesh):
    fine = Mesh(mesh.devices.reshape(8, 4, 2, 4, 4), ("y", "zl", "c", "x", "zh"))
    in_specs = (
        P(REPLICA, TENSOR),
        P(TENSOR, None),
        P(None, REPLICA, TENSOR),
        P(None, REPLICA, TENSOR),
        P(),
        P(),
        P(REPLICA),
    )
    return jax.shard_map(body, mesh=fine, in_specs=in_specs, out_specs=P(REPLICA, TENSOR), check_vma=False)
```

```python
import jax
import jax.numpy as jnp
from jax import lax
from jax.sharding import Mesh, PartitionSpec as P

ADAPTER_RANK = 64
WORKING_SLOTS = 8
ADAPTER_SCALE = 0.5

f32 = jnp.float32
bf16 = jnp.bfloat16

REPLICA = ("y", "zl", "c")
TENSOR = ("x", "zh")


def after(value, *earlier):
    return lax.optimization_barrier((value,) + earlier)[0]


def following(value, earlier):
    first = earlier[0, 0]
    return jnp.where(first != first, jnp.nan, value).astype(value.dtype)


def picking(working_adapters, store_row, adapters):
    ids = working_adapters.reshape(-1)
    places = lax.broadcasted_iota(jnp.int32, (ids.shape[0], adapters), 1)
    rows = jnp.sum(jnp.where(ids[:, None] == places, store_row[None, :], 0), axis=1)
    return (rows[:, None] == places).astype(bf16)


def picked(pick, store):
    rows = jnp.dot(pick, store[:, 0, :], preferred_element_type=f32).astype(bf16)
    return rows.reshape(-1, WORKING_SLOTS, store.shape[2])


def sum_over(part, axis):
    size = lax.axis_size(axis)
    spread = jnp.broadcast_to(part[None], (size,) + part.shape)
    return jnp.sum(lax.all_to_all(spread, axis, split_axis=0, concat_axis=0, tiled=True), axis=0)


def shifted(value, axis, by):
    size = lax.axis_size(axis)
    return lax.ppermute(value, axis, [(i, (i + by) % size) for i in range(size)])


def body(x_block, weight, down_store, up_store, working_adapters, store_row, slot):
    rows, features = x_block.shape
    xs, zs = lax.axis_size("x"), lax.axis_size("zh")
    core, x_at, z_at = lax.axis_index("c"), lax.axis_index("x"), lax.axis_index("zh")
    half = features // 2

    def columns(x_by, z_by):
        return (lax.rem(x_at + x_by, xs) * zs + lax.rem(z_at + z_by, zs)) * features

    def weight_of(source, x_by, z_by):
        return lax.dynamic_slice(source, (core * half, columns(x_by, z_by)), (half, features))

    def product(mine, other, z_bys, w):
        partial = jnp.dot(lhs_mine, mine, preferred_element_type=f32) + jnp.dot(
            lhs_other, other, preferred_element_type=f32
        )
        parts = []
        for k, z_by in enumerate(z_bys):
            own = lax.dynamic_slice(w, (0, columns(0, z_by)), (features, features))
            own = jnp.dot(x_block, own, preferred_element_type=f32)
            parts.append(partial[:, k * features:(k + 1) * features] + own)
        return parts

    pick = picking(working_adapters, store_row, down_store.shape[0])
    outgoing = jnp.concatenate([picked(pick, down_store), picked(pick, up_store)], axis=1)
    fetched = lax.all_to_all(outgoing, REPLICA, split_axis=0, concat_axis=0, tiled=True).transpose(1, 0, 2)
    down = fetched[:WORKING_SLOTS].reshape(WORKING_SLOTS * ADAPTER_RANK, features)
    up = fetched[WORKING_SLOTS:].reshape(WORKING_SLOTS * ADAPTER_RANK, features)

    swapped = jnp.concatenate([x_block[:, half:], x_block[:, :half]], axis=1)
    ordered = after(jnp.where(core == 0, x_block, swapped), outgoing)
    got = [shifted(jnp.concatenate([ordered, weight_of(weight, by, 2)], axis=0), "x", by) for by in range(1, xs)]
    lhs_mine = jnp.concatenate([block[:rows, :half] for block in got], axis=1)
    lhs_other = jnp.concatenate([block[:rows, half:] for block in got], axis=1)
    far_mine = jnp.concatenate([block[rows:] for block in got], axis=0)
    (far,) = product(far_mine, shifted(far_mine, "c", 1), (2,), weight)
    far = far.astype(bf16)
    far_sum = shifted(far, "zh", 2)

    selector = slot[None, :] == jnp.arange(WORKING_SLOTS, dtype=jnp.int32)[:, None]
    all_ranks = lax.dot_general(down, x_block, (((1,), (1,)), ((), ())), preferred_element_type=f32)
    ranks = jnp.sum(all_ranks.reshape(WORKING_SLOTS, ADAPTER_RANK, rows) * selector.astype(f32)[:, None, :], axis=0)
    ranks = following(sum_over(ranks, "x"), far_sum)
    rounded = sum_over(ranks, "zh").astype(bf16)
    expanded = (rounded[None] * selector.astype(bf16)[:, None, :]).reshape(WORKING_SLOTS * ADAPTER_RANK, rows)

    near_weight = after(weight, far)
    near = [
        shifted(jnp.concatenate([weight_of(near_weight, by, z_by) for z_by in (1, 3, 0)], axis=1), "x", by)
        for by in range(1, xs)
    ]
    near_mine = following(after(jnp.concatenate(near, axis=0), far_sum), rounded)
    up_part, down_part, total = product(near_mine, shifted(near_mine, "c", 1), (1, 3, 0), weight)
    up_sum = shifted(up_part.astype(bf16), "zh", 1)
    down_sum = shifted(down_part.astype(bf16), "zh", 3)
    term = lax.dot_general(expanded, up, (((0,), (0,)), ((), ())), preferred_element_type=f32)
    total = total + far_sum.astype(f32) + ADAPTER_SCALE * term
    return (total + up_sum.astype(f32) + down_sum.astype(f32)).astype(bf16)


def solution(mesh):
    fine = Mesh(mesh.devices.reshape(8, 4, 2, 4, 4), ("y", "zl", "c", "x", "zh"))
    in_specs = (
        P(REPLICA, TENSOR),
        P(TENSOR, None),
        P(None, REPLICA, TENSOR),
        P(None, REPLICA, TENSOR),
        P(),
        P(),
        P(REPLICA),
    )
    return jax.shard_map(body, mesh=fine, in_specs=in_specs, out_specs=P(REPLICA, TENSOR), check_vma=False)
```

```python
import jax
import jax.numpy as jnp
from jax import lax
from jax.sharding import Mesh, PartitionSpec as P

ADAPTER_RANK = 64
WORKING_SLOTS = 8
ADAPTER_SCALE = 0.5

f32 = jnp.float32
bf16 = jnp.bfloat16

REPLICA = ("y", "zl", "c")
TENSOR = ("x", "zh")


def after(value, *earlier):
    return lax.optimization_barrier((value,) + earlier)[0]


def following(value, earlier):
    first = earlier[0, 0]
    return jnp.where(first != first, jnp.nan, value).astype(value.dtype)


def picking(working_adapters, store_row, adapters):
    ids = working_adapters.reshape(-1)
    places = lax.broadcasted_iota(jnp.int32, (ids.shape[0], adapters), 1)
    rows = jnp.sum(jnp.where(ids[:, None] == places, store_row[None, :], 0), axis=1)
    return (rows[:, None] == places).astype(bf16)


def picked(pick, store):
    rows = jnp.dot(pick, store[:, 0, :], preferred_element_type=f32).astype(bf16)
    return rows.reshape(-1, WORKING_SLOTS, store.shape[2])


def sum_over(part, axis):
    size = lax.axis_size(axis)
    spread = jnp.broadcast_to(part[None], (size,) + part.shape)
    return jnp.sum(lax.all_to_all(spread, axis, split_axis=0, concat_axis=0, tiled=True), axis=0)


def shifted(value, axis, by):
    size = lax.axis_size(axis)
    return lax.ppermute(value, axis, [(i, (i + by) % size) for i in range(size)])


def body(x_block, weight, down_store, up_store, working_adapters, store_row, slot):
    rows, features = x_block.shape
    xs, zs = lax.axis_size("x"), lax.axis_size("zh")
    core, x_at, z_at = lax.axis_index("c"), lax.axis_index("x"), lax.axis_index("zh")
    half = features // 2

    pick = picking(working_adapters, store_row, down_store.shape[0])
    outgoing = jnp.concatenate([picked(pick, down_store), picked(pick, up_store)], axis=1)
    fetched = lax.all_to_all(outgoing, REPLICA, split_axis=0, concat_axis=0, tiled=True).transpose(1, 0, 2)
    down = fetched[:WORKING_SLOTS].reshape(WORKING_SLOTS * ADAPTER_RANK, features)
    up = fetched[WORKING_SLOTS:].reshape(WORKING_SLOTS * ADAPTER_RANK, features)

    def columns(x_by, z_by):
        return (lax.rem(x_at + x_by, xs) * zs + lax.rem(z_at + z_by, zs)) * features

    swapped = jnp.concatenate([x_block[:, half:], x_block[:, :half]], axis=1)
    ordered = jnp.where(core == 0, x_block, swapped)
    runs = [slice(k * (rows // zs), (k + 1) * (rows // zs)) for k in range(zs)]
    beside = after(jnp.concatenate([ordered[run] for run in runs], axis=1), outgoing)
    halves, blocks = [], []
    for by in range(1, xs):
        begin = lax.rem(x_at + by, xs) * zs * features
        part = lax.dynamic_slice(weight, (core * half, begin), (half, zs * features))
        part = shifted(jnp.concatenate([part, beside], axis=0), "x", by)
        halves.append(part[:half])
        blocks.append(jnp.concatenate([part[half:, k * features:(k + 1) * features] for k in range(zs)], axis=0))

    selector = slot[None, :] == jnp.arange(WORKING_SLOTS, dtype=jnp.int32)[:, None]
    all_ranks = lax.dot_general(down, x_block, (((1,), (1,)), ((), ())), preferred_element_type=f32)
    ranks = jnp.sum(all_ranks.reshape(WORKING_SLOTS, ADAPTER_RANK, rows) * selector.astype(f32)[:, None, :], axis=0)
    lhs_mine = jnp.concatenate([block[:, :half] for block in blocks], axis=1)
    lhs_other = jnp.concatenate([block[:, half:] for block in blocks], axis=1)
    ranks = sum_over(ranks, "x")
    high = ranks.astype(bf16)
    low = (ranks - high.astype(f32)).astype(bf16)
    both = jnp.concatenate([high, low], axis=1)

    mine = jnp.concatenate([following(halves[0], ranks)] + halves[1:], axis=0)
    other = shifted(mine, "c", 1)

    def at(part, z_by):
        return lax.dynamic_slice(part, (0, lax.rem(z_at + z_by, zs) * features), (part.shape[0], features))

    total = None
    for z_by in (2, 1, 3, 0):
        own = lax.dynamic_slice(weight, (0, columns(0, z_by)), (features, features))
        base = jnp.dot(x_block, own, preferred_element_type=f32)
        base = base + jnp.dot(lhs_mine, at(mine, z_by), preferred_element_type=f32)
        base = base + jnp.dot(lhs_other, at(other, z_by), preferred_element_type=f32)
        if z_by:
            block = shifted(jnp.concatenate([base.astype(bf16), both], axis=0), "zh", z_by).astype(f32)
            base = block[:rows]
            ranks = ranks + (block[rows:, :rows] + block[rows:, rows:])
        total = base if total is None else total + base
    rounded = ranks.astype(bf16)
    expanded = (rounded[None] * selector.astype(bf16)[:, None, :]).reshape(WORKING_SLOTS * ADAPTER_RANK, rows)
    term = lax.dot_general(expanded, up, (((0,), (0,)), ((), ())), preferred_element_type=f32)
    return (total + ADAPTER_SCALE * term).astype(bf16)


def solution(mesh):
    fine = Mesh(mesh.devices.reshape(8, 4, 2, 4, 4), ("y", "zl", "c", "x", "zh"))
    in_specs = (
        P(REPLICA, TENSOR),
        P(TENSOR, None),
        P(None, REPLICA, TENSOR),
        P(None, REPLICA, TENSOR),
        P(),
        P(),
        P(REPLICA),
    )
    return jax.shard_map(body, mesh=fine, in_specs=in_specs, out_specs=P(REPLICA, TENSOR), check_vma=False)
```

```python
import jax
import jax.numpy as jnp
from jax import lax
from jax.sharding import Mesh, PartitionSpec as P

ADAPTER_RANK = 64
WORKING_SLOTS = 8
ADAPTER_SCALE = 0.5

f32 = jnp.float32
bf16 = jnp.bfloat16

REPLICA = ("y", "zl", "c")
TENSOR = ("x", "zh")


def after(value, *earlier):
    return lax.optimization_barrier((value,) + earlier)[0]


def following(value, earlier):
    first = earlier[0, 0]
    return jnp.where(first != first, jnp.nan, value).astype(value.dtype)


def picking(working_adapters, store_row, adapters):
    ids = working_adapters.reshape(-1)
    places = lax.broadcasted_iota(jnp.int32, (ids.shape[0], adapters), 1)
    rows = jnp.sum(jnp.where(ids[:, None] == places, store_row[None, :], 0), axis=1)
    return (rows[:, None] == places).astype(bf16)


def picked(pick, store):
    rows = jnp.dot(pick, store[:, 0, :], preferred_element_type=f32).astype(bf16)
    return rows.reshape(-1, WORKING_SLOTS, store.shape[2])


def sum_over(part, axis):
    size = lax.axis_size(axis)
    spread = jnp.broadcast_to(part[None], (size,) + part.shape)
    return jnp.sum(lax.all_to_all(spread, axis, split_axis=0, concat_axis=0, tiled=True), axis=0)


def shifted(value, axis, by):
    size = lax.axis_size(axis)
    return lax.ppermute(value, axis, [(i, (i + by) % size) for i in range(size)])


def body(x_block, weight, down_store, up_store, working_adapters, store_row, slot):
    rows, features = x_block.shape
    xs, zs = lax.axis_size("x"), lax.axis_size("zh")
    core, x_at, z_at = lax.axis_index("c"), lax.axis_index("x"), lax.axis_index("zh")
    half = features // 2

    pick = picking(working_adapters, store_row, down_store.shape[0])
    outgoing = jnp.concatenate([picked(pick, down_store), picked(pick, up_store)], axis=1)
    fetched = lax.all_to_all(outgoing, REPLICA, split_axis=0, concat_axis=0, tiled=True).transpose(1, 0, 2)
    down = fetched[:WORKING_SLOTS].reshape(WORKING_SLOTS * ADAPTER_RANK, features)
    up = fetched[WORKING_SLOTS:].reshape(WORKING_SLOTS * ADAPTER_RANK, features)

    swapped = jnp.concatenate([x_block[:, half:], x_block[:, :half]], axis=1)
    ordered = jnp.where(core == 0, x_block, swapped)
    runs = [slice(k * (rows // zs), (k + 1) * (rows // zs)) for k in range(zs)]
    beside = jnp.concatenate([ordered[run] for run in runs], axis=1)
    parts = []
    for by in range(1, xs):
        begin = lax.rem(x_at + by, xs) * zs * features
        part = lax.dynamic_slice(weight, (core * half, begin), (half, zs * features))
        parts.append(shifted(jnp.concatenate([part, beside], axis=0), "x", by))
    ahead, across, behind = parts

    def requests_of(part):
        block = jnp.concatenate([part[half:, k * features:(k + 1) * features] for k in range(zs)], axis=0)
        return block[:, :half], block[:, half:]

    def product(part):
        mine, other = requests_of(part)
        far = shifted(part, "c", 1)
        return jnp.dot(mine, part[:half], preferred_element_type=f32) + jnp.dot(
            other, far[:half], preferred_element_type=f32
        )

    own = lax.dynamic_slice(weight, (0, x_at * zs * features), (features, zs * features))
    near = jnp.dot(x_block, own, preferred_element_type=f32) + product(ahead) + product(behind)

    selector = slot[None, :] == jnp.arange(WORKING_SLOTS, dtype=jnp.int32)[:, None]
    all_ranks = lax.dot_general(down, x_block, (((1,), (1,)), ((), ())), preferred_element_type=f32)
    ranks = jnp.sum(all_ranks.reshape(WORKING_SLOTS, ADAPTER_RANK, rows) * selector.astype(f32)[:, None, :], axis=0)
    ranks = sum_over(ranks, "x")
    high = lax.reduce_precision(ranks, 8, 7)
    both = jnp.concatenate([high, ranks - high], axis=1).astype(bf16)

    across = following(following(across, near), ranks)
    other_across = shifted(across, "c", 1)
    lhs_mine, lhs_other = requests_of(across)

    def at(part, z_by, count):
        return lax.dynamic_slice(part, (0, lax.rem(z_at + z_by, zs) * features), (count, features))

    total = None
    for z_by in (2, 1, 3, 0):
        base = at(near, z_by, rows)
        base = base + jnp.dot(lhs_mine, at(across, z_by, half), preferred_element_type=f32)
        base = base + jnp.dot(lhs_other, at(other_across, z_by, half), preferred_element_type=f32)
        if z_by:
            block = shifted(jnp.concatenate([base.astype(bf16), both], axis=0), "zh", z_by).astype(f32)
            base = block[:rows]
            ranks = ranks + (block[rows:, :rows] + block[rows:, rows:])
        total = base if total is None else total + base
    rounded = ranks.astype(bf16)
    expanded = (rounded[None] * selector.astype(bf16)[:, None, :]).reshape(WORKING_SLOTS * ADAPTER_RANK, rows)
    term = lax.dot_general(expanded, up, (((0,), (0,)), ((), ())), preferred_element_type=f32)
    return (total + ADAPTER_SCALE * term).astype(bf16)


def solution(mesh):
    fine = Mesh(mesh.devices.reshape(8, 4, 2, 4, 4), ("y", "zl", "c", "x", "zh"))
    in_specs = (
        P(REPLICA, TENSOR),
        P(TENSOR, None),
        P(None, REPLICA, TENSOR),
        P(None, REPLICA, TENSOR),
        P(),
        P(),
        P(REPLICA),
    )
    return jax.shard_map(body, mesh=fine, in_specs=in_specs, out_specs=P(REPLICA, TENSOR), check_vma=False)
```

```python
import jax
import jax.numpy as jnp
from jax import lax
from jax.sharding import Mesh, PartitionSpec as P

ADAPTER_RANK = 64
WORKING_SLOTS = 8
ADAPTER_SCALE = 0.5

f32 = jnp.float32
bf16 = jnp.bfloat16

REPLICA = ("y", "zl", "c")
TENSOR = ("x", "zh")


def after(value, *earlier):
    return lax.optimization_barrier((value,) + earlier)[0]


def following(value, earlier):
    first = earlier[0, 0]
    return jnp.where(first != first, jnp.nan, value).astype(value.dtype)


def picking(working_adapters, store_row, adapters):
    ids = working_adapters.reshape(-1)
    places = lax.broadcasted_iota(jnp.int32, (ids.shape[0], adapters), 1)
    rows = jnp.sum(jnp.where(ids[:, None] == places, store_row[None, :], 0), axis=1)
    return (rows[:, None] == places).astype(bf16)


def picked(pick, store):
    rows = jnp.dot(pick, store[:, 0, :], preferred_element_type=f32).astype(bf16)
    return rows.reshape(-1, WORKING_SLOTS, store.shape[2])


def sum_over(part, axis):
    size = lax.axis_size(axis)
    spread = jnp.broadcast_to(part[None], (size,) + part.shape)
    return jnp.sum(lax.all_to_all(spread, axis, split_axis=0, concat_axis=0, tiled=True), axis=0)


def shifted(value, axis, by):
    size = lax.axis_size(axis)
    return lax.ppermute(value, axis, [(i, (i + by) % size) for i in range(size)])


def body(x_block, weight, down_store, up_store, working_adapters, store_row, slot):
    rows, features = x_block.shape
    xs, zs = lax.axis_size("x"), lax.axis_size("zh")
    core, x_at, z_at = lax.axis_index("c"), lax.axis_index("x"), lax.axis_index("zh")
    half = features // 2

    def columns(x_by, z_by):
        return (lax.rem(x_at + x_by, xs) * zs + lax.rem(z_at + z_by, zs)) * features

    def weight_of(source, x_by, z_by):
        return lax.dynamic_slice(source, (core * half, columns(x_by, z_by)), (half, features))

    def product(mine, other, z_bys, w):
        partial = jnp.dot(lhs_mine, mine, preferred_element_type=f32) + jnp.dot(
            lhs_other, other, preferred_element_type=f32
        )
        parts = []
        for k, z_by in enumerate(z_bys):
            own = lax.dynamic_slice(w, (0, columns(0, z_by)), (features, features))
            own = jnp.dot(x_block, own, preferred_element_type=f32)
            parts.append(partial[:, k * features:(k + 1) * features] + own)
        return parts

    pick = picking(working_adapters, store_row, down_store.shape[0])
    outgoing = jnp.concatenate([picked(pick, down_store), picked(pick, up_store)], axis=1)
    fetched = lax.all_to_all(outgoing, REPLICA, split_axis=0, concat_axis=0, tiled=True).transpose(1, 0, 2)
    down = fetched[:WORKING_SLOTS].reshape(WORKING_SLOTS * ADAPTER_RANK, features)
    up = fetched[WORKING_SLOTS:].reshape(WORKING_SLOTS * ADAPTER_RANK, features)

    swapped = jnp.concatenate([x_block[:, half:], x_block[:, :half]], axis=1)
    ordered = after(jnp.where(core == 0, x_block, swapped), outgoing)
    got = [shifted(jnp.concatenate([ordered, weight_of(weight, by, 2)], axis=0), "x", by) for by in range(1, xs)]
    lhs_mine = jnp.concatenate([block[:rows, :half] for block in got], axis=1)
    lhs_other = jnp.concatenate([block[:rows, half:] for block in got], axis=1)
    far_mine = jnp.concatenate([block[rows:] for block in got], axis=0)
    selector = slot[None, :] == jnp.arange(WORKING_SLOTS, dtype=jnp.int32)[:, None]
    all_ranks = lax.dot_general(down, x_block, (((1,), (1,)), ((), ())), preferred_element_type=f32)
    ranks = jnp.sum(all_ranks.reshape(WORKING_SLOTS, ADAPTER_RANK, rows) * selector.astype(f32)[:, None, :], axis=0)
    ranks = sum_over(ranks, "x")
    high = lax.reduce_precision(ranks, 8, 7)
    both = jnp.concatenate([high, ranks - high], axis=1).astype(bf16)

    def with_ranks(base):
        return jnp.concatenate([base.astype(bf16), both], axis=0)

    (far,) = product(far_mine, shifted(far_mine, "c", 1), (2,), weight)
    far = with_ranks(far)
    far_sum = shifted(far, "zh", 2)

    near_weight = after(weight, far)
    near = [
        shifted(jnp.concatenate([weight_of(near_weight, by, z_by) for z_by in (1, 3, 0)], axis=1), "x", by)
        for by in range(1, xs)
    ]
    near_mine = following(jnp.concatenate(near, axis=0), far_sum)
    up_part, down_part, total = product(near_mine, shifted(near_mine, "c", 1), (1, 3, 0), weight)
    up_sum = shifted(with_ranks(up_part), "zh", 1)
    down_sum = shifted(with_ranks(down_part), "zh", 3)
    for block in (far_sum, up_sum, down_sum):
        block = block.astype(f32)
        total = total + block[:rows]
        ranks = ranks + (block[rows:, :rows] + block[rows:, rows:])
    rounded = ranks.astype(bf16)
    expanded = (rounded[None] * selector.astype(bf16)[:, None, :]).reshape(WORKING_SLOTS * ADAPTER_RANK, rows)
    term = lax.dot_general(expanded, up, (((0,), (0,)), ((), ())), preferred_element_type=f32)
    return (total + ADAPTER_SCALE * term).astype(bf16)


def solution(mesh):
    fine = Mesh(mesh.devices.reshape(8, 4, 2, 4, 4), ("y", "zl", "c", "x", "zh"))
    in_specs = (
        P(REPLICA, TENSOR),
        P(TENSOR, None),
        P(None, REPLICA, TENSOR),
        P(None, REPLICA, TENSOR),
        P(),
        P(),
        P(REPLICA),
    )
    return jax.shard_map(body, mesh=fine, in_specs=in_specs, out_specs=P(REPLICA, TENSOR), check_vma=False)
```

```python
import jax
import jax.numpy as jnp
from jax import lax
from jax.sharding import Mesh, PartitionSpec as P

ADAPTER_RANK = 64
WORKING_SLOTS = 8
ADAPTER_SCALE = 0.5

f32 = jnp.float32
bf16 = jnp.bfloat16

REPLICA = ("y", "zl", "c")
TENSOR = ("x", "zh")


def after(value, *earlier):
    return lax.optimization_barrier((value,) + earlier)[0]


def following(value, earlier):
    first = earlier[0, 0]
    return jnp.where(first != first, jnp.nan, value).astype(value.dtype)


def picking(working_adapters, store_row, adapters):
    ids = working_adapters.reshape(-1)
    places = lax.broadcasted_iota(jnp.int32, (ids.shape[0], adapters), 1)
    rows = jnp.sum(jnp.where(ids[:, None] == places, store_row[None, :], 0), axis=1)
    return (rows[:, None] == places).astype(bf16)


def picked(pick, store):
    rows = jnp.dot(pick, store[:, 0, :], preferred_element_type=f32).astype(bf16)
    return rows.reshape(-1, WORKING_SLOTS, store.shape[2])


def sum_over(part, axis):
    size = lax.axis_size(axis)
    spread = jnp.broadcast_to(part[None], (size,) + part.shape)
    return jnp.sum(lax.all_to_all(spread, axis, split_axis=0, concat_axis=0, tiled=True), axis=0)


def shifted(value, axis, by):
    size = lax.axis_size(axis)
    return lax.ppermute(value, axis, [(i, (i + by) % size) for i in range(size)])


def body(x_block, weight, down_store, up_store, working_adapters, store_row, slot):
    rows, features = x_block.shape
    xs, zs = lax.axis_size("x"), lax.axis_size("zh")
    core, x_at, z_at = lax.axis_index("c"), lax.axis_index("x"), lax.axis_index("zh")
    half = features // 2

    def columns(x_by, z_by):
        return (lax.rem(x_at + x_by, xs) * zs + lax.rem(z_at + z_by, zs)) * features

    def weight_of(source, x_by, z_by):
        return lax.dynamic_slice(source, (core * half, columns(x_by, z_by)), (half, features))

    def product(mine, other, z_bys, w):
        partial = jnp.dot(lhs_mine, mine, preferred_element_type=f32) + jnp.dot(
            lhs_other, other, preferred_element_type=f32
        )
        parts = []
        for k, z_by in enumerate(z_bys):
            own = lax.dynamic_slice(w, (0, columns(0, z_by)), (features, features))
            own = jnp.dot(x_block, own, preferred_element_type=f32)
            parts.append(partial[:, k * features:(k + 1) * features] + own)
        return parts

    pick = picking(working_adapters, store_row, down_store.shape[0])
    outgoing = jnp.concatenate([picked(pick, down_store), picked(pick, up_store)], axis=1)
    fetched = lax.all_to_all(outgoing, REPLICA, split_axis=0, concat_axis=0, tiled=True).transpose(1, 0, 2)
    down = fetched[:WORKING_SLOTS].reshape(WORKING_SLOTS * ADAPTER_RANK, features)
    up = fetched[WORKING_SLOTS:].reshape(WORKING_SLOTS * ADAPTER_RANK, features)

    swapped = jnp.concatenate([x_block[:, half:], x_block[:, :half]], axis=1)
    ordered = after(jnp.where(core == 0, x_block, swapped), outgoing)
    got = [shifted(jnp.concatenate([ordered, weight_of(weight, by, 2)], axis=0), "x", by) for by in range(1, xs)]
    lhs_mine = jnp.concatenate([block[:rows, :half] for block in got], axis=1)
    lhs_other = jnp.concatenate([block[:rows, half:] for block in got], axis=1)
    far_mine = jnp.concatenate([block[rows:] for block in got], axis=0)
    selector = slot[None, :] == jnp.arange(WORKING_SLOTS, dtype=jnp.int32)[:, None]
    all_ranks = lax.dot_general(down, x_block, (((1,), (1,)), ((), ())), preferred_element_type=f32)
    ranks = jnp.sum(all_ranks.reshape(WORKING_SLOTS, ADAPTER_RANK, rows) * selector.astype(f32)[:, None, :], axis=0)
    ranks = sum_over(ranks, "x")
    rounded = sum_over(ranks, "zh").astype(bf16)

    (far,) = product(far_mine, shifted(far_mine, "c", 1), (2,), weight)
    far = following(far.astype(bf16), ranks)
    far_sum = shifted(far, "zh", 2)

    near_weight = after(weight, far)
    near = [
        shifted(jnp.concatenate([weight_of(near_weight, by, z_by) for z_by in (1, 3, 0)], axis=1), "x", by)
        for by in range(1, xs)
    ]
    near_mine = following(following(jnp.concatenate(near, axis=0), far_sum), rounded)
    up_part, down_part, total = product(near_mine, shifted(near_mine, "c", 1), (1, 3, 0), weight)
    up_sum = shifted(up_part.astype(bf16), "zh", 1)
    down_sum = shifted(down_part.astype(bf16), "zh", 3)
    expanded = (rounded[None] * selector.astype(bf16)[:, None, :]).reshape(WORKING_SLOTS * ADAPTER_RANK, rows)
    term = lax.dot_general(expanded, up, (((0,), (0,)), ((), ())), preferred_element_type=f32)
    total = total + far_sum.astype(f32) + ADAPTER_SCALE * term
    return (total + up_sum.astype(f32) + down_sum.astype(f32)).astype(bf16)


def solution(mesh):
    fine = Mesh(mesh.devices.reshape(8, 4, 2, 4, 4), ("y", "zl", "c", "x", "zh"))
    in_specs = (
        P(REPLICA, TENSOR),
        P(TENSOR, None),
        P(None, REPLICA, TENSOR),
        P(None, REPLICA, TENSOR),
        P(),
        P(),
        P(REPLICA),
    )
    return jax.shard_map(body, mesh=fine, in_specs=in_specs, out_specs=P(REPLICA, TENSOR), check_vma=False)
```

```python
import jax
import jax.numpy as jnp
from jax import lax
from jax.sharding import Mesh, PartitionSpec as P

ADAPTER_RANK = 64
WORKING_SLOTS = 8
ADAPTER_SCALE = 0.5
CHUNKS = ((2,), (1, 3), (0,))

f32 = jnp.float32
bf16 = jnp.bfloat16

REPLICA = ("y", "zl", "c")
TENSOR = ("x", "zh")


def fetch_adapters(down_store, up_store, working_adapters, store_row):
    groups = working_adapters.shape[0]
    adapters, _, features = down_store.shape
    ids = working_adapters.reshape(-1)
    is_adapter = ids[:, None] == lax.broadcasted_iota(jnp.int32, (ids.shape[0], adapters), 1)
    rows = jnp.sum(jnp.where(is_adapter, store_row[None, :], 0), axis=1)
    pick = (rows[:, None] == lax.broadcasted_iota(jnp.int32, (ids.shape[0], adapters), 1)).astype(bf16)
    down = jnp.dot(pick, down_store[:, 0, :], preferred_element_type=f32).astype(bf16)
    up = jnp.dot(pick, up_store[:, 0, :], preferred_element_type=f32).astype(bf16)
    outgoing = jnp.concatenate(
        [down.reshape(groups, WORKING_SLOTS, features), up.reshape(groups, WORKING_SLOTS, features)], axis=1
    )
    fetched = lax.all_to_all(outgoing, REPLICA, split_axis=0, concat_axis=0, tiled=True)
    fetched = fetched.transpose(1, 0, 2)
    down = fetched[:WORKING_SLOTS].reshape(WORKING_SLOTS * ADAPTER_RANK, features)
    up = fetched[WORKING_SLOTS:].reshape(WORKING_SLOTS * ADAPTER_RANK, features)
    return down, up


def sum_over(part, axis):
    size = lax.axis_size(axis)
    spread = jnp.broadcast_to(part[None], (size,) + part.shape)
    return jnp.sum(lax.all_to_all(spread, axis, split_axis=0, concat_axis=0, tiled=True), axis=0)


def shifted(value, axis, by):
    size = lax.axis_size(axis)
    return lax.ppermute(value, axis, [(i, (i + by) % size) for i in range(size)])


def body(x_block, weight, down_store, up_store, working_adapters, store_row, slot):
    rows, features = x_block.shape
    xs, zs = lax.axis_size("x"), lax.axis_size("zh")
    core, x_at, z_at = lax.axis_index("c"), lax.axis_index("x"), lax.axis_index("zh")
    half = features // 2

    swapped = jnp.concatenate([x_block[:, half:], x_block[:, :half]], axis=1)
    ordered = jnp.where(core == 0, x_block, swapped)
    blocks = [shifted(ordered, "x", by) for by in range(1, xs)]
    lhs_mine = jnp.concatenate([block[:, :half] for block in blocks], axis=1)
    lhs_other = jnp.concatenate([block[:, half:] for block in blocks], axis=1)

    down, up = fetch_adapters(down_store, up_store, working_adapters, store_row)
    selector = slot[None, :] == jnp.arange(WORKING_SLOTS, dtype=jnp.int32)[:, None]
    all_ranks = lax.dot_general(down, x_block, (((1,), (1,)), ((), ())), preferred_element_type=f32)
    ranks = jnp.sum(all_ranks.reshape(WORKING_SLOTS, ADAPTER_RANK, rows) * selector.astype(f32)[:, None, :], axis=0)
    ranks = sum_over(ranks, "x")
    high = lax.reduce_precision(ranks, 8, 7)
    both = jnp.concatenate([high, ranks - high], axis=1).astype(bf16)

    def columns(x_by, z_by):
        return (lax.rem(x_at + x_by, xs) * zs + lax.rem(z_at + z_by, zs)) * features

    def weight_of(z_bys, x_by):
        return jnp.concatenate(
            [lax.dynamic_slice(weight, (core * half, columns(x_by, z_by)), (half, features)) for z_by in z_bys], axis=1
        )

    total = None
    for z_bys in CHUNKS:
        mine = jnp.concatenate([shifted(weight_of(z_bys, by), "x", by) for by in range(1, xs)], axis=0)
        other = shifted(mine, "c", 1)
        partial = jnp.dot(lhs_mine, mine, preferred_element_type=f32) + jnp.dot(
            lhs_other, other, preferred_element_type=f32
        )
        for k, z_by in enumerate(z_bys):
            own = lax.dynamic_slice(weight, (0, columns(0, z_by)), (features, features))
            part = partial[:, k * features:(k + 1) * features] + jnp.dot(x_block, own, preferred_element_type=f32)
            if z_by:
                block = shifted(jnp.concatenate([part.astype(bf16), both], axis=0), "zh", z_by).astype(f32)
                part = block[:rows]
                ranks = ranks + (block[rows:, :rows] + block[rows:, rows:])
            total = part if total is None else total + part
    rounded = ranks.astype(bf16)
    expanded = (rounded[None] * selector.astype(bf16)[:, None, :]).reshape(WORKING_SLOTS * ADAPTER_RANK, rows)
    term = lax.dot_general(expanded, up, (((0,), (0,)), ((), ())), preferred_element_type=f32)
    return (total + ADAPTER_SCALE * term).astype(bf16)


def solution(mesh):
    fine = Mesh(mesh.devices.reshape(8, 4, 2, 4, 4), ("y", "zl", "c", "x", "zh"))
    in_specs = (
        P(REPLICA, TENSOR),
        P(TENSOR, None),
        P(None, REPLICA, TENSOR),
        P(None, REPLICA, TENSOR),
        P(),
        P(),
        P(REPLICA),
    )
    return jax.shard_map(body, mesh=fine, in_specs=in_specs, out_specs=P(REPLICA, TENSOR), check_vma=False)
```
